768 devices in a mesh: row: 16 (over z_hi, x, core), col: 48 (over y, z_lo).
Axes of the slice: x: 4, y: 8, z: 12 (z_hi: 2, z_lo: 6; z = z_hi * 6 + z_lo), core: 2. Of those that a mesh axis runs over, the one named last changes fastest.
Arguments:
- features: bfloat16 [48, 2048, 128], P('col', 'row'), may hold values from -6 to 6
- layer_weight: bfloat16 [128, 512], replicated, may hold values from -0.5 to 0.5
- cotangent: bfloat16 [16, 6144, 512], P('row', 'col'), may hold values from -6 to 6
- block_coords: int32 [16, 48, 32, 2], P('row', 'col'), may hold values from 0 to 47, as said below
- block_counts: int32 [16, 48], P('row', 'col'), may hold values from 1 to 32, as said below
- block_masks: int32 [16, 48, 32, 128, 128], P('row', 'col'), may hold values 0 or 1
- edge_weight: bfloat16 [16, 48, 32, 128, 128], P('row', 'col'), may hold values from 0.0099487305 to 0.06982422
Outputs:
- activated: bfloat16 [16, 6144, 512], P('row', 'col')
- feature_grad: bfloat16 [48, 2048, 128], P('col', 'row')
The draws below stay inside these ranges and needn't reach their ends.
Inputs may be any that keep to these rules, and one draw needn't show every extreme that they name: `block_coords`: within one grid cell the first block_counts slots name distinct blocks; row entries lie in 0 to 47 and column entries in 0 to 15. `block_counts`: some grid cell uses all 32 slots.
All inputs are finite; a program needn't handle non-finite values. No bound on the sum of `block_masks` on one device may be relied on, other than what follows from the above.
Results may differ from the reference program's by a relative error of at most 0.0049.
Values may be sent and summed in bfloat16 or wider, within the bound.
A program may use at most 32 MiB of HBM per device.

```python
import jax
import jax.numpy as jnp
from jax import lax

FI = 128
FO = 512
BLOCK = 128
PANEL_R = 6144
PANEL_C = 2048
BLK_R = 48
BLK_C = 16
CAP = 32
N_ROW = 16
N_COL = 48


def draw_block_coords(key, part):
    key = jax.random.fold_in(key, 11)
    cells = N_ROW * N_COL
    keys = jax.random.split(key, cells)
    spots = jax.vmap(lambda one: jax.random.permutation(one, BLK_R * BLK_C)[:CAP])(keys)
    spots = spots.astype(jnp.int32)
    coords = jnp.stack([spots // BLK_C, spots % BLK_C], axis=-1)
    return coords.reshape(N_ROW, N_COL, CAP, 2).astype(jnp.int32)


def draw_block_counts(key, part):
    key = jax.random.fold_in(key, 23)
    first, second, third = jax.random.split(key, 3)
    lowest = max(CAP // 4, 1)
    highest = max(CAP // 2, lowest) + 1
    modest = jax.random.randint(first, (N_ROW * N_COL,), lowest, highest, dtype=jnp.int32)
    fulls = jax.random.randint(second, (N_ROW * N_COL,), 0, 4, dtype=jnp.int32) == 0
    counts = jnp.where(fulls, CAP, modest).astype(jnp.int32)
    chosen = jax.random.randint(third, (), 0, N_ROW * N_COL, dtype=jnp.int32)
    counts = jnp.where(jnp.arange(N_ROW * N_COL, dtype=jnp.int32) == chosen, CAP, counts)
    return counts.reshape(N_ROW, N_COL).astype(jnp.int32)


def place_ends(result, stream_key, least, top_value):
    longest = result.shape.index(max(result.shape))
    spots = []
    for shift in (0, 1):
        where = [jax.random.randint(jax.random.fold_in(stream_key, axis), (), 0, length) for axis, length in enumerate(result.shape)]
        where[longest] = (where[longest] + shift) % result.shape[longest]
        spots.append(tuple(where))
    return result.at[spots[0]].set(least).at[spots[1]].set(top_value)


def block_scale(stream_key, shape, pieces, least, high):
    def one(dim, parts):
        heights = jax.random.uniform(jax.random.fold_in(jax.random.fold_in(stream_key, 6), dim), (parts,), jnp.float32, least / len(pieces), high / len(pieces))
        return jnp.repeat(jnp.exp(heights), shape[dim] // parts).reshape((-1,) + (1,) * (len(shape) - dim - 1))

    loudness = one(*pieces[0])
    for cut in pieces[1:]:
        loudness = loudness * one(*cut)
    return loudness


def gaussian(stream_key, dims, deviation, limit, pieces=(), held_as=jnp.bfloat16):
    array = deviation * jax.random.normal(stream_key, dims, jnp.float32)
    if pieces:
        array = array * block_scale(stream_key, dims, pieces, -0.22, 0.18)
    return jnp.clip(array, -limit, limit).astype(held_as)


def setup_inputs(seed: int = 0) -> dict:
    key_of = jax.random.split(jax.random.key(seed), 8)
    features = gaussian(key_of[0], (N_COL, PANEL_C, FI), 1.0, 6.0, ((0, 48), (1, 16)))
    layer_weight = gaussian(key_of[1], (FI, FO), FI ** -0.5, 0.5)
    cotangent = gaussian(key_of[2], (N_ROW, PANEL_R, FO), 1.0, 6.0, ((0, 16), (1, 48)))
    block_coords = draw_block_coords(jax.random.fold_in(key_of[7], 71), 0)
    block_counts = draw_block_counts(jax.random.fold_in(key_of[7], 71), 0)
    block_masks = place_ends((jax.random.randint(key_of[5], (N_ROW, N_COL, CAP, BLOCK, BLOCK), 0, 4) < 1).astype(jnp.int32), jax.random.fold_in(key_of[5], 1), 0, 1)
    edge_weight = jnp.clip(0.0099487305 + 0.05987549 * jax.random.uniform(key_of[6], (N_ROW, N_COL, CAP, BLOCK, BLOCK), jnp.float32) ** block_scale(key_of[6], (N_ROW, N_COL, CAP, BLOCK, BLOCK), ((0, 16), (1, 48)), -0.2, 0.2), 0.0099487305, 0.06982422).astype(jnp.bfloat16)
    return dict(features=features, layer_weight=layer_weight, cotangent=cotangent, block_coords=block_coords, block_counts=block_counts, block_masks=block_masks, edge_weight=edge_weight)


def activation(value):
    return jax.nn.gelu(value, approximate=True)

def reference(features, layer_weight, cotangent, block_coords, block_counts, block_masks, edge_weight):
    highest = lax.Precision.HIGHEST
    valid = jnp.arange(CAP, dtype=jnp.int32)[None, None, :] < block_counts[:, :, None]
    values = block_masks.astype(jnp.float32) * edge_weight.astype(jnp.float32)
    panels = features.astype(jnp.float32).reshape(N_COL, BLK_C, BLOCK, FI)
    col_ids = jnp.arange(N_COL, dtype=jnp.int32)
    row_ids = jnp.arange(N_ROW, dtype=jnp.int32)

    def forward_row(which):
        blocks = values[which]
        brow = block_coords[which, :, :, 0]
        bcol = block_coords[which, :, :, 1]
        taken = panels[col_ids[:, None], bcol]
        prod = jnp.einsum('ckij,ckjf->ckif', blocks, taken, precision=highest)
        onehot = ((brow[..., None] == jnp.arange(BLK_R, dtype=jnp.int32)) & valid[which][..., None]).astype(jnp.float32)
        return jnp.einsum('ckb,ckif->bif', onehot, prod, precision=highest).reshape(PANEL_R, FI)
    aggregate = lax.map(forward_row, row_ids)
    pre = jnp.einsum('rpf,fo->rpo', aggregate, layer_weight.astype(jnp.float32), precision=highest)
    outputs, pullback = jax.vjp(activation, pre)
    gain = pullback(cotangent.astype(jnp.float32))[0]
    back = jnp.einsum('rpo,fo->rpf', gain, layer_weight.astype(jnp.float32), precision=highest).astype(jnp.bfloat16)
    back_blocks = back.astype(jnp.float32).reshape(N_ROW, BLK_R, BLOCK, FI)

    def backward_col(which):
        blocks = values[:, which]
        brow = block_coords[:, which, :, 0]
        bcol = block_coords[:, which, :, 1]
        taken = back_blocks[row_ids[:, None], brow]
        prod = jnp.einsum('rkij,rkif->rkjf', blocks, taken, precision=highest)
        onehot = ((bcol[..., None] == jnp.arange(BLK_C, dtype=jnp.int32)) & valid[:, which][..., None]).astype(jnp.float32)
        return jnp.einsum('rkb,rkjf->bjf', onehot, prod, precision=highest).reshape(PANEL_C, FI)
    feature_grad = lax.map(backward_col, col_ids).astype(jnp.bfloat16)
    return (outputs.astype(jnp.bfloat16), feature_grad)
```

```python
import functools

import jax
import jax.numpy as jnp
from jax import lax
from jax.experimental import pallas as pl
from jax.experimental.pallas import tpu as pltpu
from jax.sharding import PartitionSpec as P

MESH = pl.DeviceIdType.MESH
ZH, NX, NK = 2, 4, 2
NY, NZ = 8, 6
N_ROW, N_COL = ZH * NX * NK, NY * NZ
B = 128
H = B // 2
FI, FO = 128, 512
CAP = 32
HIGHEST = lax.Precision.HIGHEST
VMEM_LIMIT = 48 * 1024 * 1024


def row_coords():
    r = lax.axis_index("row")
    return r // (NX * NK), (r // NK) % NX, r % NK


def row_id(zh, x, k):
    return (zh * NX + x) * NK + k


def barrier(peers):
    sem = pltpu.get_barrier_semaphore()
    for peer in peers:
        pl.semaphore_signal(sem, inc=1, device_id=peer, device_id_type=MESH)
    pl.semaphore_wait(sem, len(peers))


def send(src, dst, send_sem, recv_sem, peer):
    copy = pltpu.make_async_remote_copy(
        src_ref=src, dst_ref=dst, send_sem=send_sem, recv_sem=recv_sem,
        device_id=peer, device_id_type=MESH,
    )
    copy.start()
    return copy


def gather_kernel(count_ref, feat_ref, mask_ref, weight_ref, panel_ref, blocks_ref, turned_ref,
                  mbuf, wbuf, load_sem, x_send, x_recv, z_send, z_recv, c_send, c_recv):
    zh, x, k = row_coords()
    c = lax.axis_index("col")
    here = row_id(zh, x, k)
    far = row_id(1 - zh, x, k)
    z_peer = (far, c)
    c_peer = (row_id(zh, x, 1 - k), c)
    x_to = [(x + d) % NX for d in (1, 2, 3)]
    x_from = [(x + NX - d) % NX for d in (1, 2, 3)]
    barrier([z_peer, c_peer] + [(row_id(zh, t, k), c) for t in x_to])
    sends = []
    panel_ref[here] = feat_ref[0]
    own = panel_ref.at[here]
    sends.append(send(own, own, z_send, z_recv, z_peer))
    for d in (0, 2, 1):
        sends.append(send(own, own, x_send.at[0, d], x_recv.at[0, d], (row_id(zh, x_to[d], k), c)))
    sends.append(send(own, own, c_send.at[0], c_recv.at[0], c_peer))
    loads = [
        pltpu.make_async_copy(mask_ref.at[0, 0], mbuf, load_sem.at[0]),
        pltpu.make_async_copy(weight_ref.at[0, 0], wbuf, load_sem.at[1]),
    ]
    for load in loads:
        load.start()
    for load in loads:
        load.wait()
    count = count_ref[0, 0]

    def build(slot, carry):
        keep = (mbuf[slot] * (slot < count).astype(jnp.int32)) != 0
        block = jnp.where(keep, wbuf[slot].astype(jnp.float32), 0.0)
        blocks_ref[slot] = block.astype(jnp.bfloat16)
        turned_ref[slot] = block.T.astype(jnp.bfloat16)
        return carry

    def arrived(block, sem):
        pltpu.make_async_copy(panel_ref.at[block], panel_ref.at[block], sem).wait()

    lax.fori_loop(0, CAP // 2, build, 0)
    for d in (0, 2, 1):
        block = row_id(zh, x_from[d], k)
        arrived(block, x_recv.at[0, d])
        ref = panel_ref.at[block]
        sends.append(send(ref, ref, c_send.at[1 + d], c_recv.at[1 + d], c_peer))
    lax.fori_loop(CAP // 2, CAP, build, 0)
    arrived(far, z_recv)
    ref = panel_ref.at[far]
    for d in (0, 2, 1):
        sends.append(send(ref, ref, x_send.at[1, d], x_recv.at[1, d], (row_id(zh, x_to[d], k), c)))
    sends.append(send(ref, ref, c_send.at[4], c_recv.at[4], c_peer))
    for d in (0, 2, 1):
        block = row_id(1 - zh, x_from[d], k)
        arrived(block, x_recv.at[1, d])
        ref = panel_ref.at[block]
        sends.append(send(ref, ref, c_send.at[5 + d], c_recv.at[5 + d], c_peer))
    for i, (h, t) in enumerate([(zh, x)] + [(zh, t) for t in x_from] + [(1 - zh, x)] + [(1 - zh, t) for t in x_from]):
        arrived(row_id(h, t, 1 - k), c_recv.at[i])
    for copy in sends:
        copy.wait_send()


def forward_kernel(coord_ref, blocks_ref, panel_ref, out_ref, prod):
    for slot in range(CAP):
        prod[slot] = jnp.dot(blocks_ref[slot], panel_ref[coord_ref[0, 0, slot, 1]], preferred_element_type=jnp.float32)
    out_ref[...] = jnp.zeros_like(out_ref)

    def add(slot, carry):
        b = coord_ref[0, 0, slot, 0]
        out_ref[b] = out_ref[b] + prod[slot]
        return carry

    lax.fori_loop(0, CAP, add, 0)


def backward_kernel(coord_ref, turned_ref, back_ref, out_ref, prod):
    for slot in range(CAP):
        prod[slot] = jnp.dot(turned_ref[slot], back_ref[coord_ref[0, 0, slot, 0]], preferred_element_type=jnp.float32)
    out_ref[...] = jnp.zeros_like(out_ref)

    def add(slot, carry):
        b = coord_ref[0, 0, slot, 1]
        at = (b % NK) * (ZH * NX) + b // NK
        out_ref[at] = out_ref[at] + prod[slot]
        return carry

    lax.fori_loop(0, CAP, add, 0)


def layer_kernel(part_ref, w_ref, cot_ref, act_ref, back_ref, r_out, l_out, r_in, l_in, z_out, z_in, total,
                 rs, rr, ls, lr, zs, zr, grs, grr, gls, glr, gzs, gzr):
    r = lax.axis_index("row")
    c = lax.axis_index("col")
    y, z = c // NZ, c % NZ
    right = (r, ((y + 1) % NY) * NZ + z)
    left = (r, ((y + NY - 1) % NY) * NZ + z)
    barrier([right, left] + [(r, y * NZ + (z + d) % NZ) for d in range(1, NZ)])

    def wait(ref, sem):
        pltpu.make_async_copy(ref, ref, sem).wait()

    low, high = pl.ds(0, H), pl.ds(H, H)

    def part(dy, j):
        return part_ref.at[((y + dy) % NY) * NZ + (z + 1 + j) % NZ]

    def first(j, carry):
        mine = part(4, j)
        r_out[0, j, :H] = mine[:H].astype(jnp.bfloat16)
        send(r_out.at[0, j, low], r_in.at[0, j, low], rs.at[0, j], rr.at[0, j], right)
        l_out[0, j, H:] = mine[H:].astype(jnp.bfloat16)
        send(l_out.at[0, j, high], l_in.at[0, j, high], ls.at[0, j], lr.at[0, j], left)
        return carry

    def second(j, carry):
        mine = part(3, j)
        r_out[1, j, H:] = mine[H:].astype(jnp.bfloat16)
        wait(r_in.at[0, j, low], rr.at[0, j])
        r_out[1, j, :H] = (mine[:H] + r_in[0, j, :H].astype(jnp.float32)).astype(jnp.bfloat16)
        send(r_out.at[1, j], r_in.at[1, j], rs.at[1, j], rr.at[1, j], right)
        mine = part(5, j)
        l_out[1, j, :H] = mine[:H].astype(jnp.bfloat16)
        wait(l_in.at[0, j, high], lr.at[0, j])
        l_out[1, j, H:] = (mine[H:] + l_in[0, j, H:].astype(jnp.float32)).astype(jnp.bfloat16)
        send(l_out.at[1, j], l_in.at[1, j], ls.at[1, j], lr.at[1, j], left)
        return carry

    def later(s, j, carry):
        wait(r_in.at[s - 1, j], rr.at[s - 1, j])
        r_out[s, j] = (part(4 - s, j)[...] + r_in[s - 1, j].astype(jnp.float32)).astype(jnp.bfloat16)
        send(r_out.at[s, j], r_in.at[s, j], rs.at[s, j], rr.at[s, j], right)
        wait(l_in.at[s - 1, j], lr.at[s - 1, j])
        l_out[s, j] = (part(4 + s, j)[...] + l_in[s - 1, j].astype(jnp.float32)).astype(jnp.bfloat16)
        send(l_out.at[s, j], l_in.at[s, j], ls.at[s, j], lr.at[s, j], left)
        return carry

    def collect(j):
        wait(r_in.at[3, j], rr.at[3, j])
        wait(l_in.at[3, j], lr.at[3, j])
        return part(0, j)[...] + r_in[3, j].astype(jnp.float32) + l_in[3, j].astype(jnp.float32)

    def pass_on(j, carry):
        z_out[j] = collect(j).astype(jnp.bfloat16)
        send(z_out.at[j], z_in.at[j], zs.at[j], zr.at[j], (r, y * NZ + (z + 1 + j) % NZ))
        return carry

    lax.fori_loop(0, NZ, first, 0)
    lax.fori_loop(0, NZ, second, 0)
    lax.fori_loop(0, NZ, functools.partial(later, 2), 0)
    lax.fori_loop(0, NZ, functools.partial(later, 3), 0)
    lax.fori_loop(0, NZ - 1, pass_on, 0)
    total[...] = collect(NZ - 1)

    def take(j, carry):
        wait(z_in.at[j], zr.at[j])
        total[...] = total[...] + z_in[j].astype(jnp.float32)
        return carry

    lax.fori_loop(0, NZ - 1, take, 0)

    weight = w_ref[...].astype(jnp.float32)
    pre = jnp.dot(total[...], weight, precision=HIGHEST, preferred_element_type=jnp.float32)
    scale = 0.7978845608028654
    t = jnp.tanh(scale * (pre + 0.044715 * (pre * pre * pre)))
    cdf = 0.5 * (1.0 + t)
    act_ref[0] = (pre * cdf).astype(jnp.bfloat16)
    slope = cdf + pre * (0.5 * (1.0 - t * t)) * (scale * (1.0 + 3 * 0.044715 * (pre * pre)))
    gain = cot_ref[0].astype(jnp.float32) * slope
    back = lax.dot_general(gain, weight, (((1,), (1,)), ((), ())), precision=HIGHEST,
                           preferred_element_type=jnp.float32)
    back_ref[c] = back.astype(jnp.bfloat16)

    def block(dy, j):
        return back_ref.at[((y + dy) % NY) * NZ + (z + j) % NZ]

    def hop(s, j):
        if s < 3:
            ref = block(NY - s, j)
            send(ref, ref, grs.at[s, j], grr.at[s, j], right)
            ref = block(s, j)
            send(ref, ref, gls.at[s, j], glr.at[s, j], left)
        else:
            ref = block(NY - 3, j).at[low]
            send(ref, ref, grs.at[s, j], grr.at[s, j], right)
            ref = block(3, j).at[high]
            send(ref, ref, gls.at[s, j], glr.at[s, j], left)

    own = block(0, 0)
    hop(0, 0)
    for d in (1, 5, 2, 4, 3):
        send(own, own, gzs.at[d], gzr.at[d], (r, y * NZ + (z + d) % NZ))
    for d in (5, 1, 4, 2, 3):
        j = NZ - d
        wait(block(0, j), gzr.at[d])
        hop(0, j)

    def onward(s, j, carry):
        wait(block(NY - s, j), grr.at[s - 1, j])
        wait(block(s, j), glr.at[s - 1, j])
        hop(s, j)
        return carry

    for s in (1, 2, 3):
        lax.fori_loop(0, NZ, functools.partial(onward, s), 0)

    def finish(j, carry):
        wait(block(4, j).at[low], grr.at[3, j])
        wait(block(4, j).at[high], glr.at[3, j])
        return carry

    lax.fori_loop(0, NZ, finish, 0)

    def drain(j, carry):
        half = r_out.at[0, j, low]
        full = r_out.at[1, j]
        for s in range(4):
            wait(half if s == 0 else full, rs.at[s, j])
            wait(half if s == 0 else full, ls.at[s, j])
            wait(half if s == 3 else full, grs.at[s, j])
            wait(half if s == 3 else full, gls.at[s, j])
        return carry

    lax.fori_loop(0, NZ, drain, 0)
    for j in range(NZ - 1):
        wait(z_out.at[j], zs.at[j])
        wait(z_out.at[j], gzs.at[j + 1])


def scatter_kernel(part_ref, out_ref, c_in, x_out, x_in, z_out, z_in, cs, cr, xs, xr, zs, zr):
    zh, x, k = row_coords()
    c = lax.axis_index("col")
    z_peer = (row_id(1 - zh, x, k), c)
    c_peer = (row_id(zh, x, 1 - k), c)
    x_to = [(x + d) % NX for d in (1, 2, 3)]
    x_peers = [(row_id(zh, t, k), c) for t in x_to]
    barrier([z_peer, c_peer] + x_peers)
    halves = (1 - zh, zh)
    sends = []
    for i, h in enumerate(halves):
        at = pl.ds(h * NX, NX)
        sends.append(send(part_ref.at[1 - k, at], c_in.at[at], cs.at[i], cr.at[i], c_peer))
    total = None
    for i, h in enumerate(halves):
        at = c_in.at[pl.ds(h * NX, NX)]
        pltpu.make_async_copy(at, at, cr.at[i]).wait()
        for d in (1, 0, 2):
            b = h * NX + x_to[d]
            x_out[i, d] = (part_ref[k, b] + c_in[b]).astype(jnp.bfloat16)
            sends.append(send(x_out.at[i, d], x_in.at[i, d], xs.at[i, d], xr.at[i, d], x_peers[d]))
    for i, h in enumerate(halves):
        b = h * NX + x
        total = part_ref[k, b] + c_in[b]
        for d in (0, 2, 1):
            pltpu.make_async_copy(x_in.at[i, d], x_in.at[i, d], xr.at[i, d]).wait()
            total = total + x_in[i, d].astype(jnp.float32)
        if i == 0:
            z_out[...] = total.astype(jnp.bfloat16)
            sends.append(send(z_out, z_in, zs, zr, z_peer))
    pltpu.make_async_copy(z_in, z_in, zr).wait()
    out_ref[0] = (total + z_in[...].astype(jnp.float32)).astype(jnp.bfloat16)
    for copy in sends:
        copy.wait_send()


def shards(features, layer_weight, cotangent, block_coords, block_counts, block_masks, edge_weight):
    vmem = pl.BlockSpec(memory_space=pltpu.VMEM)
    smem = pl.BlockSpec(memory_space=pltpu.SMEM)
    hbm = pl.BlockSpec(memory_space=pl.ANY)
    dma = pltpu.SemaphoreType.DMA
    bf16, f32 = jnp.bfloat16, jnp.float32

    def params(**kw):
        return pltpu.CompilerParams(vmem_limit_bytes=VMEM_LIMIT, **kw)

    panel, blocks, turned = pl.pallas_call(
        gather_kernel,
        out_shape=(
            jax.ShapeDtypeStruct((N_ROW, B, FI), bf16),
            jax.ShapeDtypeStruct((CAP, B, B), bf16),
            jax.ShapeDtypeStruct((CAP, B, B), bf16),
        ),
        in_specs=[smem, vmem, hbm, hbm],
        out_specs=(vmem, vmem, vmem),
        scratch_shapes=[
            pltpu.VMEM((CAP, B, B), jnp.int32), pltpu.VMEM((CAP, B, B), bf16), dma((2,)),
            dma((2, 3)), dma((2, 3)), dma, dma, dma((8,)), dma((8,)),
        ],
        compiler_params=params(collective_id=0, has_side_effects=True),
    )(block_counts, features, block_masks, edge_weight)

    partial_value = pl.pallas_call(
        forward_kernel,
        out_shape=jax.ShapeDtypeStruct((N_COL, B, FI), f32),
        in_specs=[smem, vmem, vmem],
        out_specs=vmem,
        scratch_shapes=[pltpu.VMEM((CAP, B, FI), f32)],
        compiler_params=params(),
    )(block_coords, blocks, panel)

    activated, back = pl.pallas_call(
        layer_kernel,
        out_shape=(jax.ShapeDtypeStruct((1, B, FO), bf16), jax.ShapeDtypeStruct((N_COL, B, FI), bf16)),
        in_specs=[vmem, vmem, vmem],
        out_specs=(vmem, vmem),
        scratch_shapes=[pltpu.VMEM((4, NZ, B, FI), bf16)] * 4
        + [pltpu.VMEM((NZ, B, FI), bf16)] * 2
        + [pltpu.VMEM((B, FI), f32)]
        + [dma((4, NZ))] * 4 + [dma((NZ,))] * 2 + [dma((4, NZ))] * 4 + [dma((NZ,))] * 2,
        compiler_params=params(collective_id=1, has_side_effects=True),
    )(partial_value, layer_weight, cotangent)

    partial_grad = pl.pallas_call(
        backward_kernel,
        out_shape=jax.ShapeDtypeStruct((N_ROW, B, FI), f32),
        in_specs=[smem, vmem, vmem],
        out_specs=vmem,
        scratch_shapes=[pltpu.VMEM((CAP, B, FI), f32)],
        compiler_params=params(),
    )(block_coords, turned, back)

    grad = pl.pallas_call(
        scatter_kernel,
        out_shape=jax.ShapeDtypeStruct((1, B, FI), bf16),
        in_specs=[vmem],
        out_specs=vmem,
        scratch_shapes=[
            pltpu.VMEM((ZH * NX, B, FI), f32),
            pltpu.VMEM((2, 3, B, FI), bf16), pltpu.VMEM((2, 3, B, FI), bf16),
            pltpu.VMEM((B, FI), bf16), pltpu.VMEM((B, FI), bf16),
            dma((2,)), dma((2,)), dma((2, 3)), dma((2, 3)), dma, dma,
        ],
        compiler_params=params(collective_id=2, has_side_effects=True),
    )(partial_grad.reshape(NK, ZH * NX, B, FI))
    return activated, grad


def solution(mesh):
    return jax.shard_map(
        shards,
        mesh=mesh,
        in_specs=(
            P("col", "row", None),
            P(),
            P("row", "col", None),
            P("row", "col", None, None),
            P("row", "col"),
            P("row", "col", None, None, None),
            P("row", "col", None, None, None),
        ),
        out_specs=(P("row", "col", None), P("col", "row", None)),
        check_vma=False,
    )
```

```python
import jax
import jax.numpy as jnp
from jax import lax
from jax.experimental import pallas as pl
from jax.experimental.pallas import tpu as pltpu
from jax.sharding import PartitionSpec as P

MESH = pl.DeviceIdType.MESH
ZH, NX, NK = 2, 4, 2
NY, NZ = 8, 6
N_ROW, N_COL = ZH * NX * NK, NY * NZ
B = 128
H = B // 2
FI, FO = 128, 512
CAP = 32
STEPS = 4
HALF = STEPS * NZ - NZ // 2
HIGHEST = lax.Precision.HIGHEST
VMEM_LIMIT = 60 * 1024 * 1024
f32, bf16, i32 = jnp.float32, jnp.bfloat16, jnp.int32


def row_id(zh, x, k):
    return (zh * NX + x) * NK + k


def send(src, dst, send_sem, recv_sem, peer):
    pltpu.make_async_remote_copy(
        src_ref=src, dst_ref=dst, send_sem=send_sem, recv_sem=recv_sem,
        device_id=peer, device_id_type=MESH,
    ).start()


def wait(ref, sem):
    pltpu.make_async_copy(ref, ref, sem).wait()


def near(z, i):
    m = jnp.minimum(z, NZ - 1 - z)
    v = jnp.where(i > 2 * m, i, jnp.where(i % 2 == 1, m - (i + 1) // 2, m + i // 2))
    return jnp.where(z < NZ // 2, v, NZ - 1 - v)


def sort_tables(key, other):
    k_sub = lax.broadcasted_iota(i32, (CAP, CAP), 0)
    k_lane = lax.broadcasted_iota(i32, (CAP, CAP), 1)
    eye = k_sub == k_lane

    def upright(v):
        return jnp.sum(jnp.where(eye, jnp.broadcast_to(v, (CAP, CAP)), 0), axis=1, keepdims=True)

    key_c = upright(key)
    before = (key_c < key) | ((key_c == key) & (k_sub < k_lane))
    rank = jnp.sum(before.astype(i32), axis=0, keepdims=True)
    lanes = lax.broadcasted_iota(i32, (CAP, 128), 1)
    at = upright(rank) == lanes

    def place(col):
        return jnp.sum(jnp.where(at, col, 0), axis=0, keepdims=True)

    order = place(lax.broadcasted_iota(i32, (CAP, 128), 0))
    source = place(jnp.broadcast_to(upright(other), (CAP, 128)))
    sorted_key = place(jnp.broadcast_to(key_c, (CAP, 128)))
    start = jnp.sum((key_c < sorted_key).astype(i32), axis=0, keepdims=True)
    same = (start != lanes[:1]).astype(i32)
    below = jnp.sum((key_c < lanes).astype(i32), axis=0, keepdims=True)
    upto = jnp.sum((key_c <= lanes).astype(i32), axis=0, keepdims=True)
    last = jnp.where(upto > below, upto, 0)
    return [order, source, same, last]


def kernel(count_ref, coord_hbm, feat_hbm, w_hbm, cot_hbm, mask_hbm, weight_hbm, act_ref, grad_ref,
           panel, coord, mbuf, wbuf, blocks, wide, cot, table, tab, sums,
           r_out, l_out, r_in, l_in, z_out, z_in, back,
           stage, c_in, x_out, x_in, q_out, q_in,
           load, fs, fx, fz, fc, rs, rr, ls, lr, zs, zr, grs, grr, gls, glr, gzs, gzr, es, ec, exs, ex, ezs, ez):
    r = lax.axis_index("row")
    c = lax.axis_index("col")
    zh, x, k = r // (NX * NK), (r // NK) % NX, r % NK
    y, z = c // NZ, c % NZ
    far = row_id(1 - zh, x, k)
    z_peer = (far, c)
    c_peer = (row_id(zh, x, 1 - k), c)
    x_to = [(x + d) % NX for d in (1, 2, 3)]
    x_from = [(x + NX - d) % NX for d in (1, 2, 3)]
    x_peers = [(row_id(zh, t, k), c) for t in x_to]
    right = (r, ((y + 1) % NY) * NZ + z)
    left = (r, ((y + NY - 1) % NY) * NZ + z)
    peers = [z_peer] + x_peers + [right, left] + [(r, y * NZ + (z + d) % NZ) for d in range(1, NZ)] + [c_peer]
    gate = pltpu.get_barrier_semaphore()
    for peer in peers:
        pl.semaphore_signal(gate, inc=1, device_id=peer, device_id_type=MESH)
    local = [
        pltpu.make_async_copy(feat_hbm.at[0], panel.at[r], load.at[0]),
        pltpu.make_async_copy(coord_hbm.at[0, 0], coord, load.at[1]),
        pltpu.make_async_copy(mask_hbm.at[0, 0], mbuf, load.at[2]),
        pltpu.make_async_copy(weight_hbm.at[0, 0], wbuf, load.at[3]),
        pltpu.make_async_copy(w_hbm, wide, load.at[4]),
        pltpu.make_async_copy(cot_hbm.at[0], cot, load.at[5]),
    ]
    for copy in local:
        copy.start()
    local[0].wait()
    pl.semaphore_wait(gate, len(peers))

    own = panel.at[r]
    send(own, own, fs, fz, z_peer)
    for d in (0, 2, 1):
        send(own, own, fs, fx.at[0, d], x_peers[d])
    send(own, own, fs, fc.at[0], c_peer)

    local[1].wait()
    valid = lax.broadcasted_iota(i32, (1, CAP), 1) < count_ref[0, 0]
    brow = jnp.where(valid, coord[0:1, :], 0)
    bcol = jnp.where(valid, coord[1:2, :], 0)
    rows = sort_tables(jnp.where(valid, brow, N_COL), bcol) + sort_tables(jnp.where(valid, bcol, N_COL), brow)
    table[...] = jnp.concatenate(rows, axis=0)
    lookup = pltpu.make_async_copy(table, tab, load.at[1])
    lookup.start()
    local[2].wait()
    local[3].wait()

    def build(slot, carry):
        blocks[slot] = jnp.where(mbuf[slot] != 0, wbuf[slot].astype(f32), 0.0).astype(bf16)
        return carry

    lax.fori_loop(0, CAP // 2, build, 0)
    for d in (0, 2, 1):
        ref = panel.at[row_id(zh, x_from[d], k)]
        wait(ref, fx.at[0, d])
        send(ref, ref, fs, fc.at[1 + d], c_peer)
    lax.fori_loop(CAP // 2, CAP, build, 0)
    lookup.wait()
    sums[0] = jnp.zeros((B, FI), f32)

    ref = panel.at[far]
    wait(ref, fz)
    for d in (0, 2, 1):
        send(ref, ref, fs, fx.at[1, d], x_peers[d])
    send(ref, ref, fs, fc.at[4], c_peer)
    for d in (0, 2, 1):
        ref = panel.at[row_id(1 - zh, x_from[d], k)]
        wait(ref, fx.at[1, d])
        send(ref, ref, fs, fc.at[5 + d], c_peer)
    for i, (h, t) in enumerate([(zh, x)] + [(zh, t) for t in x_from] + [(1 - zh, x)] + [(1 - zh, t) for t in x_from]):
        wait(panel.at[row_id(h, t, 1 - k)], fc.at[i])

    def scan(at, product):
        def eight(g, run):
            for i in range(8):
                p = g * 8 + i
                new = product(tab[at, p], tab[at + 1, p])
                run = run * tab[at + 2, p].astype(f32) + new
                sums[p + 1] = run
            return run

        lax.fori_loop(0, CAP // 8, eight, jnp.zeros((B, FI), f32))

    scan(0, lambda slot, source: jnp.dot(blocks[slot], panel[source], preferred_element_type=f32))

    low, high = pl.ds(0, H), pl.ds(H, H)

    def dest(j):
        return near(z, NZ - 1 - j)

    def part(dy, j):
        return sums[tab[3, ((y + dy) % NY) * NZ + dest(j)]]

    def first(j, carry):
        mine = part(4, j).astype(bf16)
        r_out[j, :H] = mine[:H]
        send(r_out.at[j, low], r_in.at[j, low], rs, rr.at[j], right)
        l_out[j, H:] = mine[H:]
        send(l_out.at[j, high], l_in.at[j, high], ls, lr.at[j], left)
        return carry

    def second(j, carry):
        t = NZ + j
        mine = part(3, j)
        wait(r_in.at[j, low], rr.at[j])
        r_out[t, H:] = mine[H:].astype(bf16)
        r_out[t, :H] = (mine[:H] + r_in[j, :H].astype(f32)).astype(bf16)
        send(r_out.at[t], r_in.at[t], rs, rr.at[t], right)
        mine = part(5, j)
        wait(l_in.at[j, high], lr.at[j])
        l_out[t, :H] = mine[:H].astype(bf16)
        l_out[t, H:] = (mine[H:] + l_in[j, H:].astype(f32)).astype(bf16)
        send(l_out.at[t], l_in.at[t], ls, lr.at[t], left)
        return carry

    def later(i, carry):
        s, j = 2 + i // NZ, i % NZ
        t = s * NZ + j
        wait(r_in.at[t - NZ], rr.at[t - NZ])
        r_out[t] = (part(STEPS - s, j) + r_in[t - NZ].astype(f32)).astype(bf16)
        send(r_out.at[t], r_in.at[t], rs, rr.at[t], right)
        wait(l_in.at[t - NZ], lr.at[t - NZ])
        l_out[t] = (part(STEPS + s, j) + l_in[t - NZ].astype(f32)).astype(bf16)
        send(l_out.at[t], l_in.at[t], ls, lr.at[t], left)
        return carry

    def collect(j):
        t = 3 * NZ + j
        wait(r_in.at[t], rr.at[t])
        wait(l_in.at[t], lr.at[t])
        return part(0, j) + r_in[t].astype(f32) + l_in[t].astype(f32)

    def pass_on(j, carry):
        z_out[j] = collect(j).astype(bf16)
        send(z_out.at[j], z_in.at[z], zs, zr.at[z], (r, y * NZ + dest(j)))
        return carry

    lax.fori_loop(0, NZ, first, 0)
    lax.fori_loop(0, NZ, second, 0)
    lax.fori_loop(0, 2 * NZ, later, 0)
    lax.fori_loop(0, NZ - 1, pass_on, 0)

    wait(panel.at[pl.ds(0, 15)], fs)
    wait(r_out.at[pl.ds(0, HALF)], rs)
    wait(l_out.at[pl.ds(0, HALF)], ls)
    local[4].wait()
    local[5].wait()
    weight = wide[...].astype(f32)

    def take(i, run):
        other = near(z, i)
        wait(z_in.at[other], zr.at[other])
        return run + z_in[other].astype(f32)

    total = lax.fori_loop(1, NZ, take, collect(NZ - 1))

    pre = jnp.dot(total, weight, precision=HIGHEST, preferred_element_type=f32)
    scale = 0.7978845608028654
    t = jnp.tanh(scale * (pre + 0.044715 * (pre * pre * pre)))
    cdf = 0.5 * (1.0 + t)
    slope = cdf + pre * (0.5 * (1.0 - t * t)) * (scale * (1.0 + 3 * 0.044715 * (pre * pre)))
    gain = cot[...].astype(f32) * slope
    turned = lax.dot_general(weight, gain, (((1,), (1,)), ((), ())), precision=HIGHEST, preferred_element_type=f32)
    back[c] = turned.astype(bf16)

    def block(dy, j):
        return back.at[((y + dy) % NY) * NZ + near(z, j)]

    def hop(s, j):
        t = s * NZ + j
        if s < STEPS - 1:
            right_ref, left_ref = block(NY - s, j), block(s, j)
        else:
            right_ref, left_ref = block(NY - s, j).at[low], block(s, j).at[high]
        send(right_ref, right_ref, grs, grr.at[t], right)
        send(left_ref, left_ref, gls, glr.at[t], left)

    mine = back.at[c]
    for j in range(1, NZ):
        send(mine, mine, gzs, gzr.at[z], (r, y * NZ + near(z, NZ - j)))
    act_ref[0] = (pre * cdf).astype(bf16)

    def wave(i, carry):
        for s in range(STEPS - 1, 0, -1):
            j = i - 3 * s

            @pl.when((j >= 0) & (j < NZ))
            def _():
                t = (s - 1) * NZ + j
                wait(block(NY - s, j), grr.at[t])
                wait(block(s, j), glr.at[t])
                hop(s, j)

        @pl.when((i > 0) & (i < NZ))
        def _():
            other = near(z, i)
            wait(back.at[y * NZ + other], gzr.at[other])

        @pl.when(i < NZ)
        def _():
            hop(0, i)

        return carry

    lax.fori_loop(0, NZ + 3 * (STEPS - 1), wave, 0)
    wait(z_out, zs)

    def finish(j, carry):
        t = (STEPS - 1) * NZ + j
        wait(block(STEPS, j).at[low], grr.at[t])
        wait(block(STEPS, j).at[high], glr.at[t])
        return carry

    lax.fori_loop(0, NZ, finish, 0)

    scan(4, lambda slot, source: jnp.dot(back[source], blocks[slot], preferred_element_type=f32))

    def grad(h, t, core):
        return sums[tab[7, row_id(h, t, core)]]

    halves = (1 - zh, zh)
    for i, h in enumerate(halves):
        for t in range(NX):
            stage[h * NX + t] = grad(h, t, 1 - k)
        at = pl.ds(h * NX, NX)
        send(stage.at[at], c_in.at[at], es, ec.at[i], c_peer)
    for i, h in enumerate(halves):
        wait(c_in.at[pl.ds(h * NX, NX)], ec.at[i])
        for d in (1, 0, 2):
            x_out[i * 3 + d] = (grad(h, x_to[d], k) + c_in[h * NX + x_to[d]]).astype(bf16)
            send(x_out.at[i * 3 + d], x_in.at[i * 3 + d], exs, ex.at[i * 3 + d], x_peers[d])
    for i, h in enumerate(halves):
        run = grad(h, x, k) + c_in[h * NX + x]
        for d in (0, 2, 1):
            wait(x_in.at[i * 3 + d], ex.at[i * 3 + d])
            run = run + x_in[i * 3 + d].astype(f32)
        if i == 0:
            q_out[...] = run.astype(bf16)
            send(q_out, q_in, ezs, ez, z_peer)
    wait(back.at[pl.ds(0, HALF)], grs)
    wait(back.at[pl.ds(0, HALF)], gls)
    wait(z_out, gzs)
    wait(stage, es)
    wait(x_out, exs)
    wait(q_out, ezs)
    wait(q_in, ez)
    grad_ref[0] = (run + q_in[...].astype(f32)).T.astype(bf16)


def shards(features, layer_weight, cotangent, block_coords, block_counts, block_masks, edge_weight):
    vmem = pl.BlockSpec(memory_space=pltpu.VMEM)
    smem = pl.BlockSpec(memory_space=pltpu.SMEM)
    hbm = pl.BlockSpec(memory_space=pltpu.HBM)
    dma = pltpu.SemaphoreType.DMA
    ring = pltpu.VMEM((STEPS * NZ, B, FI), bf16)
    hops = dma((STEPS * NZ,))
    return pl.pallas_call(
        kernel,
        out_shape=(jax.ShapeDtypeStruct((1, B, FO), bf16), jax.ShapeDtypeStruct((1, B, FI), bf16)),
        in_specs=[smem] + [hbm] * 6,
        out_specs=(vmem, vmem),
        scratch_shapes=[
            pltpu.VMEM((N_ROW, B, FI), bf16), pltpu.VMEM((2, CAP), i32),
            pltpu.VMEM((CAP, B, B), i32), pltpu.VMEM((CAP, B, B), bf16), pltpu.VMEM((CAP, B, B), bf16),
            pltpu.VMEM((FI, FO), bf16), pltpu.VMEM((B, FO), bf16),
            pltpu.VMEM((8, 128), i32), pltpu.SMEM((8, 128), i32), pltpu.VMEM((CAP + 1, B, FI), f32),
            ring, ring, ring, ring,
            pltpu.VMEM((NZ - 1, B, FI), bf16), pltpu.VMEM((NZ, B, FI), bf16), pltpu.VMEM((N_COL, FI, B), bf16),
            pltpu.VMEM((ZH * NX, FI, B), f32), pltpu.VMEM((ZH * NX, FI, B), f32),
            pltpu.VMEM((6, FI, B), bf16), pltpu.VMEM((6, FI, B), bf16),
            pltpu.VMEM((FI, B), bf16), pltpu.VMEM((FI, B), bf16),
            dma((6,)), dma, dma((2, 3)), dma, dma((8,)),
            dma, hops, dma, hops, dma, dma((NZ,)),
            dma, hops, dma, hops, dma, dma((NZ,)),
            dma, dma((2,)), dma, dma((6,)), dma, dma,
        ],
        compiler_params=pltpu.CompilerParams(collective_id=0, has_side_effects=True, vmem_limit_bytes=VMEM_LIMIT),
    )(block_counts, jnp.swapaxes(block_coords, 2, 3), features, layer_weight, cotangent, block_masks, edge_weight)


def solution(mesh):
    return jax.shard_map(
        shards,
        mesh=mesh,
        in_specs=(
            P("col", "row", None),
            P(),
            P("row", "col", None),
            P("row", "col", None, None),
            P("row", "col"),
            P("row", "col", None, None, None),
            P("row", "col", None, None, None),
        ),
        out_specs=(P("row", "col", None), P("col", "row", None)),
        check_vma=False,
    )
```

```python
import jax
import jax.numpy as jnp
from jax import lax
from jax.experimental import pallas as pl
from jax.experimental.pallas import tpu as pltpu
from jax.sharding import PartitionSpec as P

MESH = pl.DeviceIdType.MESH
ZH, NX, NK = 2, 4, 2
NY, NZ = 8, 6
N_ROW, N_COL = ZH * NX * NK, NY * NZ
B = 128
FI, FO = 128, 512
CAP = 32
STEPS = 4
HALF = 14
FAR = 3
WAVE = ((1, 0, 0), (1, 0, 1), (2, 3, 0), (2, 4, 0), (1, 0, 2), (2, 5, 0), (2, 3, 1), (1, 0, 3), (2, 4, 1), (2, 5, 1), (1, 0, 4))
HIGHEST = lax.Precision.HIGHEST
VMEM_LIMIT = 60 * 1024 * 1024
f32, bf16, i32 = jnp.float32, jnp.bfloat16, jnp.int32


def row_id(zh, x, k):
    return (zh * NX + x) * NK + k


def send(src, dst, send_sem, recv_sem, peer):
    pltpu.make_async_remote_copy(
        src_ref=src, dst_ref=dst, send_sem=send_sem, recv_sem=recv_sem,
        device_id=peer, device_id_type=MESH,
    ).start()


def wait(ref, sem):
    pltpu.make_async_copy(ref, ref, sem).wait()


def near(z, i):
    m = jnp.minimum(z, NZ - 1 - z)
    v = jnp.where(i > 2 * m, i, jnp.where(i % 2 == 1, m - (i + 1) // 2, m + i // 2))
    return jnp.where(z < NZ // 2, v, NZ - 1 - v)


def sort_tables(key, other):
    k_sub = lax.broadcasted_iota(i32, (CAP, CAP), 0)
    k_lane = lax.broadcasted_iota(i32, (CAP, CAP), 1)
    eye = k_sub == k_lane

    def upright(v):
        return jnp.sum(jnp.where(eye, jnp.broadcast_to(v, (CAP, CAP)), 0), axis=1, keepdims=True)

    key_c = upright(key)
    before = (key_c < key) | ((key_c == key) & (k_sub < k_lane))
    rank = jnp.sum(before.astype(i32), axis=0, keepdims=True)
    lanes = lax.broadcasted_iota(i32, (CAP, 128), 1)
    at = upright(rank) == lanes

    def place(col):
        return jnp.sum(jnp.where(at, col, 0), axis=0, keepdims=True)

    order = place(lax.broadcasted_iota(i32, (CAP, 128), 0))
    source = place(jnp.broadcast_to(upright(other), (CAP, 128)))
    sorted_key = place(jnp.broadcast_to(key_c, (CAP, 128)))
    start = jnp.sum((key_c < sorted_key).astype(i32), axis=0, keepdims=True)
    same = (start != lanes[:1]).astype(i32)
    below = jnp.sum((key_c < lanes).astype(i32), axis=0, keepdims=True)
    upto = jnp.sum((key_c <= lanes).astype(i32), axis=0, keepdims=True)
    last = jnp.where(upto > below, upto, 0)
    return [order, source, same, last]


def kernel(count_ref, coord_hbm, feat_hbm, w_hbm, cot_hbm, mask_hbm, weight_hbm, act_ref, grad_ref,
           panel, coord, mbuf, wbuf, blocks, wide, cot, table, tab, sums,
           r_out, l_out, r_in, l_in, n_out, n_in, z_out, z_in, acc, back,
           stage, c_in, x_out, x_in, q_out, q_in,
           load, fs, fx, fz, fc, rs, rr, ls, lr, ns, nr, zs, zr, grs, grr, gls, glr, gns, gnr, gzs, gzr, es, ec, exs, ex, ezs, ez):
    r = lax.axis_index("row")
    c = lax.axis_index("col")
    zh, x, k = r // (NX * NK), (r // NK) % NX, r % NK
    y, z = c // NZ, c % NZ
    far = row_id(1 - zh, x, k)
    z_peer = (far, c)
    c_peer = (row_id(zh, x, 1 - k), c)
    x_to = [(x + d) % NX for d in (1, 2, 3)]
    x_from = [(x + NX - d) % NX for d in (1, 2, 3)]
    x_peers = [(row_id(zh, t, k), c) for t in x_to]
    ahead = [(r, ((y + d) % NY) * NZ + z) for d in (1, 2)]
    behind = [(r, ((y + NY - d) % NY) * NZ + z) for d in (1, 2)]
    side, m = 1 - 2 * (z // 3), jnp.minimum(z, NZ - 1 - z)
    beside = [(z + 1, z < NZ - 1), (z - 1, z > 0), (z - 2 * side, m == 2)]
    beyond = [(z + 2 * side, z >= 0), (z + 3 * side, z >= 0), (z + 4 * side, m <= 1), (z + 5 * side, m == 0)]

    def line(column):
        return (r, y * NZ + column)

    peers = [z_peer] + x_peers + ahead + behind + [(r, y * NZ + (z + d) % NZ) for d in range(1, NZ)] + [c_peer]
    gate = pltpu.get_barrier_semaphore()
    for peer in peers:
        pl.semaphore_signal(gate, inc=1, device_id=peer, device_id_type=MESH)
    local = [
        pltpu.make_async_copy(feat_hbm.at[0], panel.at[r], load.at[0]),
        pltpu.make_async_copy(coord_hbm.at[0, 0], coord, load.at[1]),
        pltpu.make_async_copy(mask_hbm.at[0, 0], mbuf, load.at[2]),
        pltpu.make_async_copy(weight_hbm.at[0, 0], wbuf, load.at[3]),
        pltpu.make_async_copy(w_hbm, wide, load.at[4]),
        pltpu.make_async_copy(cot_hbm.at[0], cot, load.at[5]),
    ]
    for copy in local:
        copy.start()
    local[0].wait()
    pl.semaphore_wait(gate, len(peers))

    own = panel.at[r]
    send(own, own, fs, fz, z_peer)
    for d in (0, 2, 1):
        send(own, own, fs, fx.at[0, d], x_peers[d])
    send(own, own, fs, fc.at[0], c_peer)

    local[1].wait()
    valid = lax.broadcasted_iota(i32, (1, CAP), 1) < count_ref[0, 0]
    brow = jnp.where(valid, coord[0:1, :], 0)
    bcol = jnp.where(valid, coord[1:2, :], 0)
    rows = sort_tables(jnp.where(valid, brow, N_COL), bcol) + sort_tables(jnp.where(valid, bcol, N_COL), brow)
    table[...] = jnp.concatenate(rows, axis=0)
    lookup = pltpu.make_async_copy(table, tab, load.at[1])
    lookup.start()
    local[2].wait()
    local[3].wait()

    def build(slot, carry):
        blocks[slot] = jnp.where(mbuf[slot] != 0, wbuf[slot].astype(f32), 0.0).astype(bf16)
        return carry

    lax.fori_loop(0, CAP // 2, build, 0)
    for d in (0, 2, 1):
        ref = panel.at[row_id(zh, x_from[d], k)]
        wait(ref, fx.at[0, d])
        send(ref, ref, fs, fc.at[1 + d], c_peer)
    lax.fori_loop(CAP // 2, CAP, build, 0)
    lookup.wait()
    sums[0] = jnp.zeros((B, FI), f32)

    ref = panel.at[far]
    wait(ref, fz)
    for d in (0, 2, 1):
        send(ref, ref, fs, fx.at[1, d], x_peers[d])
    send(ref, ref, fs, fc.at[4], c_peer)
    for d in (0, 2, 1):
        ref = panel.at[row_id(1 - zh, x_from[d], k)]
        wait(ref, fx.at[1, d])
        send(ref, ref, fs, fc.at[5 + d], c_peer)
    for i, (h, t) in enumerate([(zh, x)] + [(zh, t) for t in x_from] + [(1 - zh, x)] + [(1 - zh, t) for t in x_from]):
        wait(panel.at[row_id(h, t, 1 - k)], fc.at[i])

    def scan(at, product):
        def eight(g, run):
            for i in range(8):
                p = g * 8 + i
                new = product(tab[at, p], tab[at + 1, p])
                run = run * tab[at + 2, p].astype(f32) + new
                sums[p + 1] = run
            return run

        lax.fori_loop(0, CAP // 8, eight, jnp.zeros((B, FI), f32))

    scan(0, lambda slot, source: jnp.dot(blocks[slot], panel[source], preferred_element_type=f32))

    def mine(dy, column):
        return sums[tab[3, ((y + dy) % NY) * NZ + column]]

    def joined(dy):
        acc[...] = mine(dy, z)
        for other, there in beside:

            @pl.when(there)
            def _():
                q = other * NY + dy
                wait(n_in.at[q], nr.at[q])
                acc[...] = acc[...] + n_in[q].astype(f32)

        return acc[...]

    def ring(way):
        return (r_out, r_in, rs, rr, ahead[0]) if way == 0 else (l_out, l_in, ls, lr, behind[0])

    def hop(way, t, u):
        out, arrive, out_sem, in_sem, peer = ring(way)
        dy = STEPS - t if way == 0 else STEPS + t
        run = joined(dy) if u == FAR else mine(dy, near(z, NZ - 1 - u))
        p, q = (t - 1) * (FAR + 1) + u, t * (FAR + 1) + u
        if t > (0 if way == u % 2 else 1):
            wait(arrive.at[p], in_sem.at[p])
            run = run + arrive[p].astype(f32)
        out[q] = run.astype(bf16)
        send(out.at[q], arrive.at[q], out_sem, in_sem.at[q], peer)

    def stage_of(i, u):
        hop(u % 2, i, u)
        if i < STEPS - 1:
            hop(1 - u % 2, i + 1, u)

    def collect(u, run):
        q = (STEPS - 1) * (FAR + 1) + u
        wait(r_in.at[q], rr.at[q])
        wait(l_in.at[q], lr.at[q])
        return run + r_in[q].astype(f32) + l_in[q].astype(f32)

    for u in range(FAR):
        stage_of(0, u)
    for n, dy in enumerate((4, 3, 5, 2, 6, 1, 7, 0)):
        for i in (2, 1):
            q = 2 * n + i - 1
            n_out[q] = mine(dy, near(z, i)).astype(bf16)
            send(n_out.at[q], n_in.at[z * NY + dy], ns, nr.at[z * NY + dy], line(near(z, i)))
    for i in range(1, STEPS):
        for u in range(FAR):
            stage_of(i, u)
        stage_of(i - 1, FAR)
    for u in range(FAR):
        z_out[u] = collect(u, mine(0, near(z, NZ - 1 - u))).astype(bf16)
        send(z_out.at[u], z_in.at[z], zs, zr.at[z], line(near(z, NZ - 1 - u)))
    stage_of(STEPS - 1, FAR)

    wait(panel.at[pl.ds(0, 15)], fs)
    wait(n_out, ns)
    wait(r_out.at[pl.ds(0, HALF)], rs)
    wait(l_out.at[pl.ds(0, HALF)], ls)
    local[4].wait()
    local[5].wait()
    weight = wide[...].astype(f32)
    acc[...] = collect(FAR, joined(0))
    for other, there in beyond:

        @pl.when(there)
        def _():
            wait(z_in.at[other], zr.at[other])
            acc[...] = acc[...] + z_in[other].astype(f32)

    total = acc[...]

    pre = jnp.dot(total, weight, precision=HIGHEST, preferred_element_type=f32)
    scale = 0.7978845608028654
    t = jnp.tanh(scale * (pre + 0.044715 * (pre * pre * pre)))
    cdf = 0.5 * (1.0 + t)
    slope = cdf + pre * (0.5 * (1.0 - t * t)) * (scale * (1.0 + 3 * 0.044715 * (pre * pre)))
    gain = cot[...].astype(f32) * slope
    turned = lax.dot_general(weight, gain, (((1,), (1,)), ((), ())), precision=HIGHEST, preferred_element_type=f32)
    back[c] = turned.astype(bf16)

    def block(dy, j):
        return back.at[((y + dy) % NY) * NZ + near(z, j)]

    def forward(way, d, tag, j):
        ref = block(NY - (tag - d), j) if way == 0 else block(tag - d, j)
        sems = (grs, grr) if way == 0 else (gls, glr)
        send(ref, ref, sems[0], sems[1].at[(tag - 1) * NZ + j], (ahead if way == 0 else behind)[d - 1])

    def arrived(way, tag, j):
        wait(block(NY - tag, j) if way == 0 else block(tag, j), (grr if way == 0 else glr).at[(tag - 1) * NZ + j])

    def share(dy):
        at = ((y + dy) % NY) * NZ + z
        for i, (other, there) in enumerate(beside):

            @pl.when(there)
            def _():
                send(back.at[at], back.at[at], gns.at[i], gnr.at[at], line(other))

    for step, j, s in WAVE:
        long_way = j % 2
        if s == 0 and j > 0:
            other = near(z, j)
            wait(back.at[y * NZ + other], gzr.at[other])
        for way in (long_way, 1 - long_way):
            reach = STEPS if way == long_way else STEPS - 1
            if step == 1:
                if 0 < s <= reach:
                    arrived(way, s, j)
                if s < reach:
                    forward(way, 1, s + 1, j)
            elif s == 0:
                forward(way, 2, 2, j)
                forward(way, 1, 1, j)
            else:
                arrived(way, 2, j)
                if reach == STEPS:
                    forward(way, 2, 4, j)
                forward(way, 1, 3, j)
        if j == 0:
            if s == 0:
                for i in (3, 2, 1, 0):
                    other, there = beyond[i]

                    @pl.when(there)
                    def _():
                        send(back.at[c], back.at[c], gzs.at[i], gzr.at[z], line(other))

            share(NY - s)
            if 0 < s < STEPS:
                share(s)
            if s == 0:
                act_ref[0] = (pre * cdf).astype(bf16)
    wait(z_out, zs)
    for j in range(FAR, NZ):
        for way in (j % 2, 1 - j % 2):
            arrived(way, 1, j)
            arrived(way, 3, j)
        arrived(j % 2, 4, j)
    for i in (1, 2):
        for t in range(NY):
            at = t * NZ + near(z, i)
            wait(back.at[at], gnr.at[at])

    scan(4, lambda slot, source: jnp.dot(back[source], blocks[slot], preferred_element_type=f32))

    def grad(h, t, core):
        return sums[tab[7, row_id(h, t, core)]]

    halves = (1 - zh, zh)
    for i, h in enumerate(halves):
        for t in range(NX):
            stage[h * NX + t] = grad(h, t, 1 - k)
        at = pl.ds(h * NX, NX)
        send(stage.at[at], c_in.at[at], es, ec.at[i], c_peer)
    for i, h in enumerate(halves):
        wait(c_in.at[pl.ds(h * NX, NX)], ec.at[i])
        for d in (1, 0, 2):
            x_out[i * 3 + d] = (grad(h, x_to[d], k) + c_in[h * NX + x_to[d]]).astype(bf16)
            send(x_out.at[i * 3 + d], x_in.at[i * 3 + d], exs, ex.at[i * 3 + d], x_peers[d])
    for i, h in enumerate(halves):
        run = grad(h, x, k) + c_in[h * NX + x]
        for d in (0, 2, 1):
            wait(x_in.at[i * 3 + d], ex.at[i * 3 + d])
            run = run + x_in[i * 3 + d].astype(f32)
        if i == 0:
            q_out[...] = run.astype(bf16)
            send(q_out, q_in, ezs, ez, z_peer)
    wait(back.at[pl.ds(0, HALF)], grs)
    wait(back.at[pl.ds(0, HALF)], gls)
    for i, (other, there) in enumerate(beside):

        @pl.when(there)
        def _():
            wait(back.at[pl.ds(0, NY)], gns.at[i])

    for i, (other, there) in enumerate(beyond):

        @pl.when(there)
        def _():
            wait(back.at[0], gzs.at[i])

    wait(stage, es)
    wait(x_out, exs)
    wait(q_out, ezs)
    wait(q_in, ez)
    grad_ref[0] = (run + q_in[...].astype(f32)).T.astype(bf16)


def shards(features, layer_weight, cotangent, block_coords, block_counts, block_masks, edge_weight):
    vmem = pl.BlockSpec(memory_space=pltpu.VMEM)
    smem = pl.BlockSpec(memory_space=pltpu.SMEM)
    hbm = pl.BlockSpec(memory_space=pltpu.HBM)
    dma = pltpu.SemaphoreType.DMA
    ring = pltpu.VMEM((STEPS * (FAR + 1), B, FI), bf16)
    hop = dma((STEPS * (FAR + 1),))
    hop_back = dma((STEPS * NZ,))
    return pl.pallas_call(
        kernel,
        out_shape=(jax.ShapeDtypeStruct((1, B, FO), bf16), jax.ShapeDtypeStruct((1, B, FI), bf16)),
        in_specs=[smem] + [hbm] * 6,
        out_specs=(vmem, vmem),
        scratch_shapes=[
            pltpu.VMEM((N_ROW, B, FI), bf16), pltpu.VMEM((2, CAP), i32),
            pltpu.VMEM((CAP, B, B), i32), pltpu.VMEM((CAP, B, B), bf16), pltpu.VMEM((CAP, B, B), bf16),
            pltpu.VMEM((FI, FO), bf16), pltpu.VMEM((B, FO), bf16),
            pltpu.VMEM((8, 128), i32), pltpu.SMEM((8, 128), i32), pltpu.VMEM((CAP + 1, B, FI), f32),
            ring, ring, ring, ring,
            pltpu.VMEM((2 * NY, B, FI), bf16), pltpu.VMEM((N_COL, B, FI), bf16), pltpu.VMEM((FAR, B, FI), bf16),
            pltpu.VMEM((NZ, B, FI), bf16), pltpu.VMEM((B, FI), f32), pltpu.VMEM((N_COL, FI, B), bf16),
            pltpu.VMEM((ZH * NX, FI, B), f32), pltpu.VMEM((ZH * NX, FI, B), f32),
            pltpu.VMEM((6, FI, B), bf16), pltpu.VMEM((6, FI, B), bf16),
            pltpu.VMEM((FI, B), bf16), pltpu.VMEM((FI, B), bf16),
            dma((6,)), dma, dma((2, 3)), dma, dma((8,)),
            dma, hop, dma, hop, dma, dma((N_COL,)), dma, dma((NZ,)),
            dma, hop_back, dma, hop_back, dma((3,)), dma((N_COL,)), dma((4,)), dma((NZ,)),
            dma, dma((2,)), dma, dma((6,)), dma, dma,
        ],
        compiler_params=pltpu.CompilerParams(collective_id=0, has_side_effects=True, vmem_limit_bytes=VMEM_LIMIT),
    )(block_counts, jnp.swapaxes(block_coords, 2, 3), features, layer_weight, cotangent, block_masks, edge_weight)


def solution(mesh):
    return jax.shard_map(
        shards,
        mesh=mesh,
        in_specs=(
            P("col", "row", None),
            P(),
            P("row", "col", None),
            P("row", "col", None, None),
            P("row", "col"),
            P("row", "col", None, None, None),
            P("row", "col", None, None, None),
        ),
        out_specs=(P("row", "col", None), P("col", "row", None)),
        check_vma=False,
    )
```

```python
import jax
import jax.numpy as jnp
from jax import lax
from jax.experimental import pallas as pl
from jax.experimental.pallas import tpu as pltpu
from jax.sharding import PartitionSpec as P

MESH = pl.DeviceIdType.MESH
ZH, NX, NK = 2, 4, 2
NY, NZ = 8, 6
N_ROW, N_COL = ZH * NX * NK, NY * NZ
B = 128
FI, FO = 128, 512
CAP = 32
STEPS = 4
HALF = 14
FAR = 3
WAVE = ((1, 0, 0), (1, 0, 1), (2, 3, 0), (2, 4, 0), (1, 0, 2), (2, 5, 0), (2, 3, 1), (1, 0, 3), (2, 4, 1), (2, 5, 1), (1, 0, 4))
HIGHEST = lax.Precision.HIGHEST
VMEM_LIMIT = 537 * 1024 * 1024 // 10
f32, bf16, i32 = jnp.float32, jnp.bfloat16, jnp.int32


def row_id(zh, x, k):
    return (zh * NX + x) * NK + k


def send(src, dst, send_sem, recv_sem, peer):
    pltpu.make_async_remote_copy(
        src_ref=src, dst_ref=dst, send_sem=send_sem, recv_sem=recv_sem,
        device_id=peer, device_id_type=MESH,
    ).start()


def wait(ref, sem):
    pltpu.make_async_copy(ref, ref, sem).wait()


def near(z, i):
    m = jnp.minimum(z, NZ - 1 - z)
    v = jnp.where(i > 2 * m, i, jnp.where(i % 2 == 1, m - (i + 1) // 2, m + i // 2))
    return jnp.where(z < NZ // 2, v, NZ - 1 - v)


def sort_tables(key, other):
    k_sub = lax.broadcasted_iota(i32, (CAP, CAP), 0)
    k_lane = lax.broadcasted_iota(i32, (CAP, CAP), 1)
    eye = k_sub == k_lane

    def upright(v):
        return jnp.sum(jnp.where(eye, jnp.broadcast_to(v, (CAP, CAP)), 0), axis=1, keepdims=True)

    key_c = upright(key)
    before = (key_c < key) | ((key_c == key) & (k_sub < k_lane))
    rank = jnp.sum(before.astype(i32), axis=0, keepdims=True)
    lanes = lax.broadcasted_iota(i32, (CAP, 128), 1)
    at = upright(rank) == lanes

    def place(col):
        return jnp.sum(jnp.where(at, col, 0), axis=0, keepdims=True)

    order = place(lax.broadcasted_iota(i32, (CAP, 128), 0))
    source = place(jnp.broadcast_to(upright(other), (CAP, 128)))
    sorted_key = place(jnp.broadcast_to(key_c, (CAP, 128)))
    start = jnp.sum((key_c < sorted_key).astype(i32), axis=0, keepdims=True)
    same = (start != lanes[:1]).astype(i32)
    below = jnp.sum((key_c < lanes).astype(i32), axis=0, keepdims=True)
    upto = jnp.sum((key_c <= lanes).astype(i32), axis=0, keepdims=True)
    last = jnp.where(upto > below, upto, 0)
    return [order, source, same, last]


def kernel(count_ref, coord_hbm, feat_hbm, w_hbm, cot_hbm, mask_hbm, weight_hbm, act_ref, grad_ref,
           panel, coord, mbuf, wbuf, blocks, wide, cot, table, tab, sums,
           r_out, l_out, r_in, l_in, n_out, n_in, z_out, z_in, acc, back,
           stage, c_in, x_out, x_in, q_out, q_in,
           load, fs, fx, fz, fc, rs, rr, ls, lr, ns, nr, zs, zr, grs, grr, gls, glr, gns, gnr, gzs, gzr, es, ec, exs, ex, ezs, ez):
    r = lax.axis_index("row")
    c = lax.axis_index("col")
    zh, x, k = r // (NX * NK), (r // NK) % NX, r % NK
    y, z = c // NZ, c % NZ
    far = row_id(1 - zh, x, k)
    z_peer = (far, c)
    c_peer = (row_id(zh, x, 1 - k), c)
    x_to = [(x + d) % NX for d in (1, 2, 3)]
    x_from = [(x + NX - d) % NX for d in (1, 2, 3)]
    x_peers = [(row_id(zh, t, k), c) for t in x_to]
    ahead = [(r, ((y + d) % NY) * NZ + z) for d in (1, 2)]
    behind = [(r, ((y + NY - d) % NY) * NZ + z) for d in (1, 2)]
    side, m = 1 - 2 * (z // 3), jnp.minimum(z, NZ - 1 - z)
    beside = [(z + 1, z < NZ - 1), (z - 1, z > 0), (z - 2 * side, m == 2)]
    beyond = [(z + 2 * side, z >= 0), (z + 3 * side, z >= 0), (z + 4 * side, m <= 1), (z + 5 * side, m == 0)]

    def line(column):
        return (r, y * NZ + column)

    peers = [z_peer] + x_peers + ahead + behind + [(r, y * NZ + (z + d) % NZ) for d in range(1, NZ)] + [c_peer]
    gate = pltpu.get_barrier_semaphore()
    for peer in peers:
        pl.semaphore_signal(gate, inc=1, device_id=peer, device_id_type=MESH)
    local = [
        pltpu.make_async_copy(feat_hbm.at[0], panel.at[r], load.at[0]),
        pltpu.make_async_copy(coord_hbm.at[0, 0], coord, load.at[1]),
        pltpu.make_async_copy(mask_hbm.at[0, 0], mbuf, load.at[2]),
        pltpu.make_async_copy(weight_hbm.at[0, 0], wbuf, load.at[3]),
        pltpu.make_async_copy(w_hbm, wide, load.at[4]),
        pltpu.make_async_copy(cot_hbm.at[0], cot, load.at[5]),
    ]
    for copy in local:
        copy.start()
    local[0].wait()
    pl.semaphore_wait(gate, len(peers))

    own = panel.at[r]
    send(own, own, fs, fz, z_peer)
    for d in (0, 2, 1):
        send(own, own, fs, fx.at[0, d], x_peers[d])
    send(own, own, fs, fc.at[0], c_peer)

    local[1].wait()
    valid = lax.broadcasted_iota(i32, (1, CAP), 1) < count_ref[0, 0]
    brow = jnp.where(valid, coord[0:1, :], 0)
    bcol = jnp.where(valid, coord[1:2, :], 0)
    rows = sort_tables(jnp.where(valid, brow, N_COL), bcol) + sort_tables(jnp.where(valid, bcol, N_COL), brow)
    table[...] = jnp.concatenate(rows, axis=0)
    lookup = pltpu.make_async_copy(table, tab, load.at[1])
    lookup.start()
    local[2].wait()
    local[3].wait()

    def build(slot, carry):
        blocks[slot] = jnp.where(mbuf[slot] != 0, wbuf[slot].astype(f32), 0.0).astype(bf16)
        return carry

    lax.fori_loop(0, CAP // 2, build, 0)
    for d in (0, 2, 1):
        ref = panel.at[row_id(zh, x_from[d], k)]
        wait(ref, fx.at[0, d])
        send(ref, ref, fs, fc.at[1 + d], c_peer)
    lax.fori_loop(CAP // 2, CAP, build, 0)
    lookup.wait()
    sums[0] = jnp.zeros((B, FI), f32)

    ref = panel.at[far]
    wait(ref, fz)
    for d in (0, 2, 1):
        send(ref, ref, fs, fx.at[1, d], x_peers[d])
    send(ref, ref, fs, fc.at[4], c_peer)
    for d in (0, 2, 1):
        ref = panel.at[row_id(1 - zh, x_from[d], k)]
        wait(ref, fx.at[1, d])
        send(ref, ref, fs, fc.at[5 + d], c_peer)
    for i, (h, t) in enumerate([(zh, x)] + [(zh, t) for t in x_from] + [(1 - zh, x)] + [(1 - zh, t) for t in x_from]):
        wait(panel.at[row_id(h, t, 1 - k)], fc.at[i])

    def scan(at, product):
        def eight(g, run):
            for i in range(8):
                p = g * 8 + i
                new = product(tab[at, p], tab[at + 1, p])
                run = run * tab[at + 2, p].astype(f32) + new
                sums[p + 1] = run
            return run

        lax.fori_loop(0, CAP // 8, eight, jnp.zeros((B, FI), f32))

    scan(0, lambda slot, source: jnp.dot(blocks[slot], panel[source], preferred_element_type=f32))

    def mine(dy, column):
        return sums[tab[3, ((y + dy) % NY) * NZ + column]]

    def joined(dy):
        acc[...] = mine(dy, z)
        for other, there in beside:

            @pl.when(there)
            def _():
                q = other * NY + dy
                wait(n_in.at[q], nr.at[q])
                acc[...] = acc[...] + n_in[q].astype(f32)

        return acc[...]

    def ring(way):
        return (r_out, r_in, rs, rr, ahead[0]) if way == 0 else (l_out, l_in, ls, lr, behind[0])

    def hop(way, t, u):
        out, arrive, out_sem, in_sem, peer = ring(way)
        dy = STEPS - t if way == 0 else STEPS + t
        run = joined(dy) if u == FAR else mine(dy, near(z, NZ - 1 - u))
        p, q = (t - 1) * (FAR + 1) + u, t * (FAR + 1) + u
        if t > (0 if way == u % 2 else 1):
            wait(arrive.at[p], in_sem.at[p])
            run = run + arrive[p].astype(f32)
        out[q] = run.astype(bf16)
        send(out.at[q], arrive.at[q], out_sem, in_sem.at[q], peer)

    def stage_of(i, u):
        hop(u % 2, i, u)
        if i < STEPS - 1:
            hop(1 - u % 2, i + 1, u)

    def collect(u, run):
        q = (STEPS - 1) * (FAR + 1) + u
        wait(r_in.at[q], rr.at[q])
        wait(l_in.at[q], lr.at[q])
        return run + r_in[q].astype(f32) + l_in[q].astype(f32)

    for u in range(FAR):
        stage_of(0, u)
    for n, dy in enumerate((4, 3, 5, 2, 6, 1, 7, 0)):
        for i in (2, 1):
            q = 2 * n + i - 1
            n_out[q] = mine(dy, near(z, i)).astype(bf16)
            send(n_out.at[q], n_in.at[z * NY + dy], ns, nr.at[z * NY + dy], line(near(z, i)))
    for i in range(1, STEPS):
        for u in range(FAR):
            stage_of(i, u)
        stage_of(i - 1, FAR)
    for u in range(FAR):
        z_out[u] = collect(u, mine(0, near(z, NZ - 1 - u))).astype(bf16)
        send(z_out.at[u], z_in.at[z], zs, zr.at[z], line(near(z, NZ - 1 - u)))
    stage_of(STEPS - 1, FAR)

    wait(panel.at[pl.ds(0, 15)], fs)
    wait(n_out, ns)
    wait(r_out.at[pl.ds(0, HALF)], rs)
    wait(l_out.at[pl.ds(0, HALF)], ls)
    local[4].wait()
    local[5].wait()
    weight = wide[...].astype(f32)
    acc[...] = collect(FAR, joined(0))
    for other, there in beyond:

        @pl.when(there)
        def _():
            wait(z_in.at[other], zr.at[other])
            acc[...] = acc[...] + z_in[other].astype(f32)

    total = acc[...]

    pre = jnp.dot(total, weight, precision=HIGHEST, preferred_element_type=f32)
    scale = 0.7978845608028654
    t = jnp.tanh(scale * (pre + 0.044715 * (pre * pre * pre)))
    cdf = 0.5 * (1.0 + t)
    slope = cdf + pre * (0.5 * (1.0 - t * t)) * (scale * (1.0 + 3 * 0.044715 * (pre * pre)))
    gain = cot[...].astype(f32) * slope
    turned = lax.dot_general(weight, gain, (((1,), (1,)), ((), ())), precision=HIGHEST, preferred_element_type=f32)
    back[c] = turned.astype(bf16)

    def block(dy, j):
        return back.at[((y + dy) % NY) * NZ + near(z, j)]

    def forward(way, d, tag, j):
        ref = block(NY - (tag - d), j) if way == 0 else block(tag - d, j)
        sems = (grs, grr) if way == 0 else (gls, glr)
        send(ref, ref, sems[0], sems[1].at[(tag - 1) * NZ + j], (ahead if way == 0 else behind)[d - 1])

    def arrived(way, tag, j):
        wait(block(NY - tag, j) if way == 0 else block(tag, j), (grr if way == 0 else glr).at[(tag - 1) * NZ + j])

    def share(dy):
        at = ((y + dy) % NY) * NZ + z
        for i, (other, there) in enumerate(beside):

            @pl.when(there)
            def _():
                send(back.at[at], back.at[at], gns.at[i], gnr.at[at], line(other))

    for step, j, s in WAVE:
        long_way = j % 2
        if s == 0 and j > 0:
            other = near(z, j)
            wait(back.at[y * NZ + other], gzr.at[other])
        for way in (long_way, 1 - long_way):
            reach = STEPS if way == long_way else STEPS - 1
            if step == 1:
                if 0 < s <= reach:
                    arrived(way, s, j)
                if s < reach:
                    forward(way, 1, s + 1, j)
            elif s == 0:
                forward(way, 2, 2, j)
                forward(way, 1, 1, j)
            else:
                arrived(way, 2, j)
                if reach == STEPS:
                    forward(way, 2, 4, j)
                forward(way, 1, 3, j)
        if j == 0:
            if s == 0:
                for i in (3, 2, 1, 0):
                    other, there = beyond[i]

                    @pl.when(there)
                    def _():
                        send(back.at[c], back.at[c], gzs.at[i], gzr.at[z], line(other))

            share(NY - s)
            if 0 < s < STEPS:
                share(s)
            if s == 0:
                act_ref[0] = (pre * cdf).astype(bf16)
    wait(z_out, zs)
    for j in range(FAR, NZ):
        for way in (j % 2, 1 - j % 2):
            arrived(way, 1, j)
            arrived(way, 3, j)
        arrived(j % 2, 4, j)
    for i in (1, 2):
        for t in range(NY):
            at = t * NZ + near(z, i)
            wait(back.at[at], gnr.at[at])

    scan(4, lambda slot, source: jnp.dot(back[source], blocks[slot], preferred_element_type=f32))

    def grad(h, t, core):
        return sums[tab[7, row_id(h, t, core)]]

    halves = (1 - zh, zh)
    for i, h in enumerate(halves):
        for t in range(NX):
            stage[h * NX + t] = grad(h, t, 1 - k).astype(bf16)
        at = pl.ds(h * NX, NX)
        send(stage.at[at], c_in.at[at], es, ec.at[i], c_peer)
    for i, h in enumerate(halves):
        wait(c_in.at[pl.ds(h * NX, NX)], ec.at[i])
        for d in (1, 0, 2):
            x_out[i * 3 + d] = (grad(h, x_to[d], k) + c_in[h * NX + x_to[d]].astype(f32)).astype(bf16)
            send(x_out.at[i * 3 + d], x_in.at[i * 3 + d], exs, ex.at[i * 3 + d], x_peers[d])
    for i, h in enumerate(halves):
        run = grad(h, x, k) + c_in[h * NX + x].astype(f32)
        for d in (0, 2, 1):
            wait(x_in.at[i * 3 + d], ex.at[i * 3 + d])
            run = run + x_in[i * 3 + d].astype(f32)
        if i == 0:
            q_out[...] = run.astype(bf16)
            send(q_out, q_in, ezs, ez, z_peer)
    wait(back.at[pl.ds(0, HALF)], grs)
    wait(back.at[pl.ds(0, HALF)], gls)
    for i, (other, there) in enumerate(beside):

        @pl.when(there)
        def _():
            wait(back.at[pl.ds(0, NY)], gns.at[i])

    for i, (other, there) in enumerate(beyond):

        @pl.when(there)
        def _():
            wait(back.at[0], gzs.at[i])

    wait(stage, es)
    wait(x_out, exs)
    wait(q_out, ezs)
    wait(q_in, ez)
    grad_ref[0] = (run + q_in[...].astype(f32)).T.astype(bf16)


def shards(features, layer_weight, cotangent, block_coords, block_counts, block_masks, edge_weight):
    vmem = pl.BlockSpec(memory_space=pltpu.VMEM)
    smem = pl.BlockSpec(memory_space=pltpu.SMEM)
    hbm = pl.BlockSpec(memory_space=pltpu.HBM)
    dma = pltpu.SemaphoreType.DMA
    ring = pltpu.VMEM((STEPS * (FAR + 1), B, FI), bf16)
    hop = dma((STEPS * (FAR + 1),))
    hop_back = dma((STEPS * NZ,))
    return pl.pallas_call(
        kernel,
        out_shape=(jax.ShapeDtypeStruct((1, B, FO), bf16), jax.ShapeDtypeStruct((1, B, FI), bf16)),
        in_specs=[smem] + [hbm] * 6,
        out_specs=(vmem, vmem),
        scratch_shapes=[
            pltpu.VMEM((N_ROW, B, FI), bf16), pltpu.VMEM((2, CAP), i32),
            pltpu.VMEM((CAP, B, B), i32), pltpu.VMEM((CAP, B, B), bf16), pltpu.VMEM((CAP, B, B), bf16),
            pltpu.VMEM((FI, FO), bf16), pltpu.VMEM((B, FO), bf16),
            pltpu.VMEM((8, 128), i32), pltpu.SMEM((8, 128), i32), pltpu.VMEM((CAP + 1, B, FI), f32),
            ring, ring, ring, ring,
            pltpu.VMEM((2 * NY, B, FI), bf16), pltpu.VMEM((N_COL, B, FI), bf16), pltpu.VMEM((FAR, B, FI), bf16),
            pltpu.VMEM((NZ, B, FI), bf16), pltpu.VMEM((B, FI), f32), pltpu.VMEM((N_COL, FI, B), bf16),
            pltpu.VMEM((ZH * NX, FI, B), bf16), pltpu.VMEM((ZH * NX, FI, B), bf16),
            pltpu.VMEM((6, FI, B), bf16), pltpu.VMEM((6, FI, B), bf16),
            pltpu.VMEM((FI, B), bf16), pltpu.VMEM((FI, B), bf16),
            dma((6,)), dma, dma((2, 3)), dma, dma((8,)),
            dma, hop, dma, hop, dma, dma((N_COL,)), dma, dma((NZ,)),
            dma, hop_back, dma, hop_back, dma((3,)), dma((N_COL,)), dma((4,)), dma((NZ,)),
            dma, dma((2,)), dma, dma((6,)), dma, dma,
        ],
        compiler_params=pltpu.CompilerParams(collective_id=0, has_side_effects=True, vmem_limit_bytes=VMEM_LIMIT),
    )(block_counts, jnp.swapaxes(block_coords, 2, 3), features, layer_weight, cotangent, block_masks, edge_weight)


def solution(mesh):
    return jax.shard_map(
        shards,
        mesh=mesh,
        in_specs=(
            P("col", "row", None),
            P(),
            P("row", "col", None),
            P("row", "col", None, None),
            P("row", "col"),
            P("row", "col", None, None, None),
            P("row", "col", None, None, None),
        ),
        out_specs=(P("row", "col", None), P("col", "row", None)),
        check_vma=False,
    )
```
